32 devices in a mesh: group: 2 (over y), row: 8 (over z, x), epoch: 2 (over core).
Axes of the slice: x: 2, y: 2, z: 4, core: 2. Of those that a mesh axis runs over, the one named last changes fastest.
Arguments:
- images: bfloat16 [8, 2048, 2048], P(('group', 'epoch'), 'row'), parts along dimension 0, may hold values from -6 to 6
- rate_vectors: int32 [2, 2], replicated, may hold values from -192 to 192
- epoch_times: int32 [4], replicated, may hold values from 0 to 127
Outputs:
- rate_images: float32 [4, 2048, 2048], P(('group', 'epoch'), 'row'), parts along dimension 0
The draws below stay inside these ranges and needn't reach their ends.
There are 2 independent parts, one for each index of `group`. The reference program is written for one: setup_inputs(seed, part) draws one part's arguments, and reference() takes and returns one part's arrays. A program takes and returns all parts, laid end to end along the dimension named above; an argument that names none is the same for every part. Nothing has to cross between parts.
All inputs are finite; a program needn't handle non-finite values.
Results may differ from the reference program's by a relative error of at most 0.011.
Values may be sent and summed in bfloat16 or wider, within the bound.
A program may use at most 128 MiB of HBM per device.

```python
import math
import jax
import jax.numpy as jnp

N = 2048
SUBPIX = 16
EPOCHS = 4
RATES = 2


def plant(values, own_key, smallest, high):
    dims = values.shape
    spot = [jax.random.randint(jax.random.fold_in(own_key, axis), (), 0, dims[axis]) for axis in range(len(dims))]
    values = values.at[tuple(spot)].set(smallest)
    longest = dims.index(max(dims))
    spot[longest] = (spot[longest] + 1) % dims[longest]
    return values.at[tuple(spot)].set(high)


def levels(rng, extent, pieces, smallest, top_value):
    loudness, own = 1.0, jax.random.fold_in(rng, 6)
    for position, parts in pieces:
        heights = jnp.exp(jax.random.uniform(jax.random.fold_in(own, position), (parts,), jnp.float32, smallest / len(pieces), top_value / len(pieces)))
        loudness = loudness * jnp.repeat(heights, extent[position] // parts).reshape([-1 if axis == position else 1 for axis in range(len(extent))])
    return loudness


def bell_draw(rng, dims, deviation, bound, split=(), held_as=jnp.bfloat16):
    array = jax.random.normal(rng, dims, jnp.float32) * deviation
    if len(split) > 0:
        array = levels(rng, dims, split, -0.22, 0.18) * array
    return jnp.clip(array, min=-bound, max=bound).astype(held_as)


def setup_inputs(seed: int = 0, part: int = 0) -> dict:
    splits = jax.random.split(jax.random.key(seed), 4)
    part_splits = jax.random.split(jax.random.fold_in(splits[3], part), 4)
    images = bell_draw(part_splits[0], (EPOCHS, N, N), 1.0, 6.0, ((0, 2), (1, 8)))
    rate_vectors = plant(jax.random.randint(splits[1], (RATES, 2), -192, 193), jax.random.fold_in(splits[1], 1), -192, 192).astype(jnp.int32)
    epoch_times = plant(jax.random.randint(splits[2], (EPOCHS,), 0, 128), jax.random.fold_in(splits[2], 1), 0, 127).astype(jnp.int32)
    return dict(images=images, rate_vectors=rate_vectors, epoch_times=epoch_times)


def dft_tables(length):
    positions = jnp.arange(length, dtype=jnp.int32)
    turn_count = positions[:, None] * positions[None, :] % length
    angles = turn_count.astype(jnp.float32) * (2.0 * math.pi / length)
    factor = 1.0 / math.sqrt(length)
    return ((jnp.cos(angles) * factor).astype(jnp.bfloat16), (jnp.sin(angles) * factor).astype(jnp.bfloat16))

def reference(images, rate_vectors, epoch_times):
    cosine, sine = dft_tables(N)
    flattened = images.reshape(EPOCHS * N, N)
    row_re = jnp.dot(flattened, cosine, preferred_element_type=jnp.float32).astype(jnp.bfloat16).reshape(EPOCHS, N, N)
    row_im = (-jnp.dot(flattened, sine, preferred_element_type=jnp.float32)).astype(jnp.bfloat16).reshape(EPOCHS, N, N)
    spec_re_list = []
    spec_im_list = []
    for epoch_pos in range(EPOCHS):
        part_re = jnp.dot(cosine, row_re[epoch_pos], preferred_element_type=jnp.float32) + jnp.dot(sine, row_im[epoch_pos], preferred_element_type=jnp.float32)
        part_im = jnp.dot(cosine, row_im[epoch_pos], preferred_element_type=jnp.float32) - jnp.dot(sine, row_re[epoch_pos], preferred_element_type=jnp.float32)
        spec_re_list.append(part_re.astype(jnp.bfloat16).astype(jnp.float32))
        spec_im_list.append(part_im.astype(jnp.bfloat16).astype(jnp.float32))
    period = SUBPIX * N
    freq_index = jnp.arange(N, dtype=jnp.int32)
    shift_y = rate_vectors[:, 0:1] * epoch_times[None, :] % period
    shift_x = rate_vectors[:, 1:2] * epoch_times[None, :] % period
    stack_scale = 1.0 / math.sqrt(EPOCHS)
    outputs = []
    for rate_pos in range(RATES):
        summed_re = jnp.zeros((N, N), jnp.float32)
        summed_im = jnp.zeros((N, N), jnp.float32)
        for epoch_pos in range(EPOCHS):
            row_turns = freq_index * shift_y[rate_pos, epoch_pos] % period
            col_turns = freq_index * shift_x[rate_pos, epoch_pos] % period
            row_angles = row_turns.astype(jnp.float32) * (2.0 * math.pi / period)
            col_angles = col_turns.astype(jnp.float32) * (2.0 * math.pi / period)
            row_cos = jnp.cos(row_angles)[:, None]
            row_sin = jnp.sin(row_angles)[:, None]
            col_cos = jnp.cos(col_angles)[None, :]
            col_sin = jnp.sin(col_angles)[None, :]
            ramp_re = col_cos * row_cos - col_sin * row_sin
            ramp_im = col_sin * row_cos + col_cos * row_sin
            summed_re = summed_re + (spec_re_list[epoch_pos] * ramp_re - spec_im_list[epoch_pos] * ramp_im)
            summed_im = summed_im + (spec_re_list[epoch_pos] * ramp_im + spec_im_list[epoch_pos] * ramp_re)
        rate_re = (summed_re * stack_scale).astype(jnp.bfloat16)
        rate_im = (summed_im * stack_scale).astype(jnp.bfloat16)
        back_re = (jnp.dot(cosine, rate_re, preferred_element_type=jnp.float32) - jnp.dot(sine, rate_im, preferred_element_type=jnp.float32)).astype(jnp.bfloat16)
        back_im = (jnp.dot(cosine, rate_im, preferred_element_type=jnp.float32) + jnp.dot(sine, rate_re, preferred_element_type=jnp.float32)).astype(jnp.bfloat16)
        picture = jnp.dot(back_re, cosine, preferred_element_type=jnp.float32) - jnp.dot(back_im, sine, preferred_element_type=jnp.float32)
        outputs.append(picture)
    return jnp.stack(outputs)
```

```python
import functools
import math

import jax
import jax.numpy as jnp
import ml_dtypes
import numpy as np
from jax import lax
from jax.sharding import PartitionSpec as P

SUBPIX = 16


@functools.lru_cache(maxsize=None)
def real_table(length):
    half = length // 2
    positions = np.arange(length, dtype=np.int64)
    turns = (positions[:half, None] * positions[None, :]) % length
    angles = turns * (2.0 * math.pi / length)
    factor = 1.0 / math.sqrt(length)
    nyquist = 1.0 - 2.0 * (positions % 2)
    table = np.concatenate([np.cos(angles), nyquist[None], np.sin(angles)[1:]]) * factor
    return table.astype(np.float32).astype(ml_dtypes.bfloat16)


def lane_order(length, devices):
    half = length // 2
    slots = np.arange(half).reshape(devices, 1, half // devices)
    return np.concatenate([slots, slots + half], axis=1).reshape(-1)


def turn_cos_sin(turns, period):
    angles = (turns % period).astype(jnp.float32) * (2.0 * math.pi / period)
    return jnp.cos(angles), jnp.sin(angles)


def coefficients(rate_vectors, epoch_times, first_slot, slots, length):
    period = SUBPIX * length
    half = length // 2
    scale = 1.0 / math.sqrt(epoch_times.shape[0])
    shift_y = rate_vectors[:, 0:1] * epoch_times[None, :] % period
    shift_x = rate_vectors[:, 1:2] * epoch_times[None, :] % period
    freq = jnp.arange(half, dtype=jnp.int32)
    row_cos, row_sin = turn_cos_sin((freq - half) * shift_y[:, :, None], period)
    row_cos = jnp.where(freq == 0, 1.0, 2.0 * row_cos)
    row_sin = jnp.where(freq == 0, 0.0, 2.0 * row_sin)
    slot = first_slot + jnp.arange(slots, dtype=jnp.int32)
    col_cos, col_sin = turn_cos_sin((slot - half) * shift_x[:, :, None], period)
    both = turn_cos_sin(shift_y + shift_x, 2 * SUBPIX)[0][:, :, None]
    only_y = turn_cos_sin(shift_y, 2 * SUBPIX)[0][:, :, None]
    only_x = turn_cos_sin(shift_x, 2 * SUBPIX)[0][:, :, None]
    zero = slot == 0
    same_re = jnp.where(zero, only_y, 2.0 * both * col_cos) * scale
    same_im = jnp.where(zero, both, 2.0 * both * col_cos) * scale
    cross = jnp.where(zero, 0.0, 2.0 * both * col_sin) * scale
    first_re = jnp.where(zero, 1.0, 2.0 * only_x * col_cos) * scale
    first_im = jnp.where(zero, only_x, 2.0 * only_x * col_cos) * scale
    first_cross = jnp.where(zero, 0.0, 2.0 * only_x * col_sin) * scale
    lanes = jnp.concatenate
    same = lanes([same_re, same_im], axis=2)
    swap = lanes([cross, -cross], axis=2)
    first_same = lanes([first_re, first_im], axis=2)
    first_swap = lanes([first_cross, -first_cross], axis=2)
    return row_cos, row_sin, same, swap, first_same, first_swap


def local(images, rate_vectors, epoch_times):
    loc_epochs, loc_rows, length = images.shape
    row_count = lax.axis_size("row")
    epoch_count = lax.axis_size("epoch")
    devices = row_count * epoch_count
    place = lax.axis_index("row") * epoch_count + lax.axis_index("epoch")
    lanes = length // devices
    slots = lanes // 2
    half = length // 2
    rates = rate_vectors.shape[0]
    table = real_table(length)
    lane_table = table[lane_order(length, devices)]
    rowwise = jnp.asarray(np.ascontiguousarray(lane_table.T))
    inverse = jnp.asarray(lane_table).reshape(devices, lanes, length)
    forward = jnp.asarray(table)
    spectrum = jnp.einsum("erc,cl->erl", images, rowwise, preferred_element_type=jnp.float32)
    spectrum = spectrum.astype(jnp.bfloat16).reshape(loc_epochs, loc_rows, devices, lanes)
    sent = spectrum.transpose(2, 0, 1, 3)
    got = lax.all_to_all(sent, ("row", "epoch"), split_axis=0, concat_axis=0, tiled=True)
    got = got.reshape(row_count, epoch_count * loc_epochs, loc_rows, lanes)
    pairs = jnp.einsum(
        "uir,ierl->eul",
        forward.reshape(length, row_count, loc_rows),
        got,
        preferred_element_type=jnp.float32,
    )
    row_cos, row_sin, same, swap, first_same, first_swap = coefficients(
        rate_vectors, epoch_times, place * slots, slots, length
    )
    even, odd = pairs[:, :half], pairs[:, half:]
    swapped = lambda a: jnp.concatenate([a[..., slots:], a[..., :slots]], axis=-1)
    row_cos, row_sin = row_cos[..., None], row_sin[..., None]
    moved_even = row_cos * even[None] + row_sin * odd[None]
    moved_odd = row_cos * odd[None] - row_sin * even[None]
    first = (jnp.arange(half) == 0)[None, None, :, None]
    same_even = jnp.where(first, first_same[:, :, None], same[:, :, None])
    swap_even = jnp.where(first, first_swap[:, :, None], swap[:, :, None])
    sum_even = jnp.sum(same_even * moved_even + swap_even * swapped(moved_even), axis=1)
    sum_odd = jnp.sum(same[:, :, None] * moved_odd + swap[:, :, None] * swapped(moved_odd), axis=1)
    stacked = jnp.concatenate([sum_even, sum_odd], axis=1).astype(jnp.bfloat16)
    back = jnp.einsum("ur,kul->krl", forward, stacked, preferred_element_type=jnp.float32)
    back = back.astype(jnp.bfloat16)
    back = back.reshape(epoch_count, rates // epoch_count, row_count, loc_rows, lanes)
    back = back.transpose(2, 0, 1, 3, 4).reshape(devices, rates // epoch_count, loc_rows, lanes)
    returned = lax.all_to_all(back, ("row", "epoch"), split_axis=0, concat_axis=0, tiled=True)
    return jnp.einsum("dkrl,dlc->krc", returned, inverse, preferred_element_type=jnp.float32)


def solution(mesh):
    in_specs = (P(("group", "epoch"), "row", None), P(), P())
    out_specs = P(("group", "epoch"), "row", None)
    return jax.shard_map(local, mesh=mesh, in_specs=in_specs, out_specs=out_specs, check_vma=False)
```

```python
import functools
import math

import jax
import jax.numpy as jnp
import ml_dtypes
import numpy as np
from jax import lax
from jax.sharding import PartitionSpec as P

SUBPIX = 16


@functools.lru_cache(maxsize=None)
def real_table(length):
    half = length // 2
    positions = np.arange(length, dtype=np.int64)
    turns = (positions[:half, None] * positions[None, :]) % length
    angles = turns * (2.0 * math.pi / length)
    factor = 1.0 / math.sqrt(length)
    nyquist = 1.0 - 2.0 * (positions % 2)
    table = np.concatenate([np.cos(angles), nyquist[None], np.sin(angles)[1:]]) * factor
    return table.astype(np.float32).astype(ml_dtypes.bfloat16)


def lane_order(length, devices):
    half = length // 2
    slots = np.arange(half).reshape(devices, 1, half // devices)
    return np.concatenate([slots, slots + half], axis=1).reshape(-1)


def turn_cos_sin(turns, period):
    angles = (turns % period).astype(jnp.float32) * (2.0 * math.pi / period)
    return jnp.cos(angles), jnp.sin(angles)


def coefficients(rate_vectors, epoch_times, first_slot, slots, length):
    period = SUBPIX * length
    half = length // 2
    scale = 1.0 / math.sqrt(epoch_times.shape[0])
    shift_y = rate_vectors[:, 0:1] * epoch_times[None, :] % period
    shift_x = rate_vectors[:, 1:2] * epoch_times[None, :] % period
    freq = jnp.arange(half, dtype=jnp.int32)
    row_cos, row_sin = turn_cos_sin((freq - half) * shift_y[:, :, None], period)
    row_cos = jnp.where(freq == 0, 1.0, 2.0 * row_cos)
    row_sin = jnp.where(freq == 0, 0.0, 2.0 * row_sin)
    slot = first_slot + jnp.arange(slots, dtype=jnp.int32)
    col_cos, col_sin = turn_cos_sin((slot - half) * shift_x[:, :, None], period)
    both = turn_cos_sin(shift_y + shift_x, 2 * SUBPIX)[0][:, :, None]
    only_y = turn_cos_sin(shift_y, 2 * SUBPIX)[0][:, :, None]
    only_x = turn_cos_sin(shift_x, 2 * SUBPIX)[0][:, :, None]
    zero = slot == 0
    same_re = jnp.where(zero, only_y, 2.0 * both * col_cos) * scale
    same_im = jnp.where(zero, both, 2.0 * both * col_cos) * scale
    cross = jnp.where(zero, 0.0, 2.0 * both * col_sin) * scale
    first_re = jnp.where(zero, 1.0, 2.0 * only_x * col_cos) * scale
    first_im = jnp.where(zero, only_x, 2.0 * only_x * col_cos) * scale
    first_cross = jnp.where(zero, 0.0, 2.0 * only_x * col_sin) * scale
    lanes = jnp.concatenate
    same = lanes([same_re, same_im], axis=2)
    swap = lanes([cross, -cross], axis=2)
    first_same = lanes([first_re, first_im], axis=2)
    first_swap = lanes([first_cross, -first_cross], axis=2)
    return row_cos, row_sin, same, swap, first_same, first_swap


def local(images, rate_vectors, epoch_times):
    loc_epochs, loc_rows, length = images.shape
    row_count = lax.axis_size("row")
    epoch_count = lax.axis_size("epoch")
    devices = row_count * epoch_count
    place = lax.axis_index("row") * epoch_count + lax.axis_index("epoch")
    lanes = length // devices
    slots = lanes // 2
    half = length // 2
    rates = rate_vectors.shape[0]
    table = real_table(length)
    lane_table = table[lane_order(length, devices)]
    rowwise = jnp.asarray(np.ascontiguousarray(lane_table.T))
    inverse = jnp.asarray(lane_table).reshape(devices, lanes, length)
    forward = jnp.asarray(table)
    table_blocks = forward.reshape(length, row_count, loc_rows)
    parts = []
    for epoch in range(loc_epochs):
        spectrum = jnp.einsum(
            "rc,cl->rl", images[epoch], rowwise, preferred_element_type=jnp.float32
        )
        sent = spectrum.astype(jnp.bfloat16).reshape(loc_rows, devices, lanes).transpose(1, 0, 2)
        got = lax.all_to_all(sent, ("row", "epoch"), split_axis=0, concat_axis=0, tiled=True)
        got = got.reshape(row_count, epoch_count, loc_rows, lanes)
        parts.append(
            jnp.einsum("uir,ijrl->jul", table_blocks, got, preferred_element_type=jnp.float32)
        )
    row_cos, row_sin, same, swap, first_same, first_swap = coefficients(
        rate_vectors, epoch_times, place * slots, slots, length
    )
    swapped = lambda a: jnp.concatenate([a[..., slots:], a[..., :slots]], axis=-1)
    row_cos, row_sin = row_cos[..., None], row_sin[..., None]
    swap, first_swap = swapped(swap), swapped(first_swap)
    sums = [0.0] * 6
    for epoch, pairs in enumerate(parts):
        for source in range(epoch_count):
            at = source * loc_epochs + epoch
            even, odd = pairs[source, :half][None], pairs[source, half:][None]
            moved_even = row_cos[:, at] * even + row_sin[:, at] * odd
            moved_odd = row_cos[:, at] * odd - row_sin[:, at] * even
            terms = (
                same[:, at, None] * moved_even,
                swap[:, at, None] * moved_even,
                same[:, at, None] * moved_odd,
                swap[:, at, None] * moved_odd,
                first_same[:, at, None] * even[:, :1],
                first_swap[:, at, None] * even[:, :1],
            )
            sums = [total + term for total, term in zip(sums, terms)]
    first = (jnp.arange(half) == 0)[None, :, None]
    sum_even = jnp.where(first, sums[4] + swapped(sums[5]), sums[0] + swapped(sums[1]))
    sum_odd = sums[2] + swapped(sums[3])
    stacked = jnp.concatenate([sum_even, sum_odd], axis=1).astype(jnp.bfloat16)
    half_rows = loc_rows // 2
    halves = table.reshape(length, row_count, 2, half_rows)
    results = []
    for part in range(2):
        columns = jnp.asarray(np.ascontiguousarray(halves[:, :, part]).reshape(length, -1))
        back = jnp.einsum("ur,kul->krl", columns, stacked, preferred_element_type=jnp.float32)
        back = back.astype(jnp.bfloat16)
        back = back.reshape(epoch_count, rates // epoch_count, row_count, half_rows, lanes)
        back = back.transpose(2, 0, 1, 3, 4)
        back = back.reshape(devices, rates // epoch_count, half_rows, lanes)
        returned = lax.all_to_all(back, ("row", "epoch"), split_axis=0, concat_axis=0, tiled=True)
        results.append(
            jnp.einsum("dkrl,dlc->krc", returned, inverse, preferred_element_type=jnp.float32)
        )
    return jnp.concatenate(results, axis=1)


def solution(mesh):
    in_specs = (P(("group", "epoch"), "row", None), P(), P())
    out_specs = P(("group", "epoch"), "row", None)
    return jax.shard_map(local, mesh=mesh, in_specs=in_specs, out_specs=out_specs, check_vma=False)
```

```python
import functools
import math

import jax
import jax.numpy as jnp
import ml_dtypes
import numpy as np
from jax import lax
from jax.experimental import pallas as pl
from jax.experimental.pallas import tpu as pltpu
from jax.sharding import PartitionSpec as P

SUBPIX = 16


@functools.lru_cache(maxsize=None)
def real_table(length):
    half = length // 2
    positions = np.arange(length, dtype=np.int64)
    turns = (positions[:half, None] * positions[None, :]) % length
    angles = turns * (2.0 * math.pi / length)
    factor = 1.0 / math.sqrt(length)
    nyquist = 1.0 - 2.0 * (positions % 2)
    table = np.concatenate([np.cos(angles), nyquist[None], np.sin(angles)[1:]]) * factor
    return table.astype(np.float32).astype(ml_dtypes.bfloat16)


def lane_order(length, devices):
    half = length // 2
    slots = np.arange(half).reshape(devices, 1, half // devices)
    return np.concatenate([slots, slots + half], axis=1).reshape(-1)


def turn_cos_sin(turns, period):
    angles = (turns % period).astype(jnp.float32) * (2.0 * math.pi / period)
    return jnp.cos(angles), jnp.sin(angles)


def coefficients(rate_vectors, epoch_times, first_slot, slots, length):
    period = SUBPIX * length
    half = length // 2
    scale = 1.0 / math.sqrt(epoch_times.shape[0])
    shift_y = rate_vectors[:, 0:1] * epoch_times[None, :] % period
    shift_x = rate_vectors[:, 1:2] * epoch_times[None, :] % period
    freq = jnp.arange(half, dtype=jnp.int32)
    row_cos, row_sin = turn_cos_sin((freq - half) * shift_y[:, :, None], period)
    row_cos = jnp.where(freq == 0, 1.0, 2.0 * row_cos)
    row_sin = jnp.where(freq == 0, 0.0, 2.0 * row_sin)
    slot = first_slot + jnp.arange(slots, dtype=jnp.int32)
    col_cos, col_sin = turn_cos_sin((slot - half) * shift_x[:, :, None], period)
    both = turn_cos_sin(shift_y + shift_x, 2 * SUBPIX)[0][:, :, None]
    only_y = turn_cos_sin(shift_y, 2 * SUBPIX)[0][:, :, None]
    only_x = turn_cos_sin(shift_x, 2 * SUBPIX)[0][:, :, None]
    zero = slot == 0
    same_re = jnp.where(zero, only_y, 2.0 * both * col_cos) * scale
    same_im = jnp.where(zero, both, 2.0 * both * col_cos) * scale
    cross = jnp.where(zero, 0.0, 2.0 * both * col_sin) * scale
    first_re = jnp.where(zero, 1.0, 2.0 * only_x * col_cos) * scale
    first_im = jnp.where(zero, only_x, 2.0 * only_x * col_cos) * scale
    first_cross = jnp.where(zero, 0.0, 2.0 * only_x * col_sin) * scale
    lanes = jnp.concatenate
    same = lanes([same_re, same_im], axis=2)
    swap = lanes([cross, -cross], axis=2)
    first_same = lanes([first_re, first_im], axis=2)
    first_swap = lanes([first_cross, -first_cross], axis=2)
    return row_cos, row_sin, same, swap, first_same, first_swap


def exchange_kernel(rows, cores, src, dst, send_sem, recv_sem, own_sem):
    count = rows * cores
    me = lax.axis_index("row") * cores + lax.axis_index("epoch")
    barrier = pltpu.get_barrier_semaphore()

    def peer(step):
        other = lax.rem(me + step, count)
        return other, {"row": lax.div(other, cores), "epoch": lax.rem(other, cores)}

    for step in range(1, count):
        pl.semaphore_signal(
            barrier, inc=1, device_id=peer(step)[1], device_id_type=pl.DeviceIdType.MESH
        )
    own = pltpu.make_async_copy(src.at[me], dst.at[me], own_sem)
    own.start()
    pl.semaphore_wait(barrier, count - 1)
    copies = []
    for step in range(1, count):
        other, device = peer(step)
        copy = pltpu.make_async_remote_copy(
            src_ref=src.at[other],
            dst_ref=dst.at[me],
            send_sem=send_sem.at[step],
            recv_sem=recv_sem.at[step],
            device_id=device,
            device_id_type=pl.DeviceIdType.MESH,
        )
        copy.start()
        copies.append(copy)
    own.wait()
    for copy in copies:
        copy.wait()


def exchange(blocks, rows, cores, identity):
    if blocks.shape[-1] % 128 or blocks.shape[-2] % 16:
        return lax.all_to_all(blocks, ("row", "epoch"), split_axis=0, concat_axis=0, tiled=True)
    return pl.pallas_call(
        functools.partial(exchange_kernel, rows, cores),
        out_shape=jax.ShapeDtypeStruct(blocks.shape, blocks.dtype),
        in_specs=[pl.BlockSpec(memory_space=pl.ANY)],
        out_specs=pl.BlockSpec(memory_space=pl.ANY),
        scratch_shapes=[
            pltpu.SemaphoreType.DMA((rows * cores,)),
            pltpu.SemaphoreType.DMA((rows * cores,)),
            pltpu.SemaphoreType.DMA,
        ],
        compiler_params=pltpu.CompilerParams(collective_id=identity, has_side_effects=True),
    )(blocks)


def local(images, rate_vectors, epoch_times):
    loc_epochs, loc_rows, length = images.shape
    row_count = lax.axis_size("row")
    epoch_count = lax.axis_size("epoch")
    devices = row_count * epoch_count
    place = lax.axis_index("row") * epoch_count + lax.axis_index("epoch")
    lanes = length // devices
    slots = lanes // 2
    half = length // 2
    rates = rate_vectors.shape[0]
    table = real_table(length)
    lane_table = table[lane_order(length, devices)]
    rowwise = jnp.asarray(np.ascontiguousarray(lane_table.T))
    inverse = jnp.asarray(lane_table).reshape(devices, lanes, length)
    forward = jnp.asarray(table)
    spectrum = jnp.einsum("erc,cl->erl", images, rowwise, preferred_element_type=jnp.float32)
    spectrum = spectrum.astype(jnp.bfloat16).reshape(loc_epochs, loc_rows, devices, lanes)
    sent = spectrum.transpose(2, 0, 1, 3)
    got = exchange(sent, row_count, epoch_count, 0)
    got = got.reshape(row_count, epoch_count * loc_epochs, loc_rows, lanes)
    pairs = jnp.einsum(
        "uir,ierl->eul",
        forward.reshape(length, row_count, loc_rows),
        got,
        preferred_element_type=jnp.float32,
    )
    row_cos, row_sin, same, swap, first_same, first_swap = coefficients(
        rate_vectors, epoch_times, place * slots, slots, length
    )
    even, odd = pairs[:, :half], pairs[:, half:]
    swapped = lambda a: jnp.concatenate([a[..., slots:], a[..., :slots]], axis=-1)
    row_cos, row_sin = row_cos[..., None], row_sin[..., None]
    moved_even = row_cos * even[None] + row_sin * odd[None]
    moved_odd = row_cos * odd[None] - row_sin * even[None]
    first = (jnp.arange(half) == 0)[None, None, :, None]
    same_even = jnp.where(first, first_same[:, :, None], same[:, :, None])
    swap_even = jnp.where(first, first_swap[:, :, None], swap[:, :, None])
    sum_even = jnp.sum(same_even * moved_even + swap_even * swapped(moved_even), axis=1)
    sum_odd = jnp.sum(same[:, :, None] * moved_odd + swap[:, :, None] * swapped(moved_odd), axis=1)
    stacked = jnp.concatenate([sum_even, sum_odd], axis=1).astype(jnp.bfloat16)
    back = jnp.einsum("ur,kul->krl", forward, stacked, preferred_element_type=jnp.float32)
    back = back.astype(jnp.bfloat16)
    back = back.reshape(epoch_count, rates // epoch_count, row_count, loc_rows, lanes)
    back = back.transpose(2, 0, 1, 3, 4).reshape(devices, rates // epoch_count, loc_rows, lanes)
    returned = exchange(back, row_count, epoch_count, 1)
    return jnp.einsum("dkrl,dlc->krc", returned, inverse, preferred_element_type=jnp.float32)


def solution(mesh):
    in_specs = (P(("group", "epoch"), "row", None), P(), P())
    out_specs = P(("group", "epoch"), "row", None)
    return jax.shard_map(local, mesh=mesh, in_specs=in_specs, out_specs=out_specs, check_vma=False)
```

```python
import functools
import math

import jax
import jax.numpy as jnp
import ml_dtypes
import numpy as np
from jax import lax
from jax.experimental import pallas as pl
from jax.experimental.pallas import tpu as pltpu
from jax.sharding import PartitionSpec as P

SUBPIX = 16


@functools.lru_cache(maxsize=None)
def real_table(length):
    half = length // 2
    positions = np.arange(length, dtype=np.int64)
    turns = (positions[:half, None] * positions[None, :]) % length
    angles = turns * (2.0 * math.pi / length)
    factor = 1.0 / math.sqrt(length)
    nyquist = 1.0 - 2.0 * (positions % 2)
    table = np.concatenate([np.cos(angles), nyquist[None], np.sin(angles)[1:]]) * factor
    return table.astype(np.float32).astype(ml_dtypes.bfloat16)


def lane_order(length, devices):
    half = length // 2
    slots = np.arange(half).reshape(devices, 1, half // devices)
    return np.concatenate([slots, slots + half], axis=1).reshape(-1)


def turn_cos_sin(turns, period):
    angles = (turns % period).astype(jnp.float32) * (2.0 * math.pi / period)
    return jnp.cos(angles), jnp.sin(angles)


def coefficients(rate_vectors, epoch_times, first_slot, slots, length):
    period = SUBPIX * length
    half = length // 2
    scale = 1.0 / math.sqrt(epoch_times.shape[0])
    shift_y = rate_vectors[:, 0:1] * epoch_times[None, :] % period
    shift_x = rate_vectors[:, 1:2] * epoch_times[None, :] % period
    freq = jnp.arange(half, dtype=jnp.int32)
    row_cos, row_sin = turn_cos_sin((freq - half) * shift_y[:, :, None], period)
    row_cos = jnp.where(freq == 0, 1.0, 2.0 * row_cos)
    row_sin = jnp.where(freq == 0, 0.0, 2.0 * row_sin)
    slot = first_slot + jnp.arange(slots, dtype=jnp.int32)
    col_cos, col_sin = turn_cos_sin((slot - half) * shift_x[:, :, None], period)
    both = turn_cos_sin(shift_y + shift_x, 2 * SUBPIX)[0][:, :, None]
    only_y = turn_cos_sin(shift_y, 2 * SUBPIX)[0][:, :, None]
    only_x = turn_cos_sin(shift_x, 2 * SUBPIX)[0][:, :, None]
    zero = slot == 0
    same_re = jnp.where(zero, only_y, 2.0 * both * col_cos) * scale
    same_im = jnp.where(zero, both, 2.0 * both * col_cos) * scale
    cross = jnp.where(zero, 0.0, 2.0 * both * col_sin) * scale
    first_re = jnp.where(zero, 1.0, 2.0 * only_x * col_cos) * scale
    first_im = jnp.where(zero, only_x, 2.0 * only_x * col_cos) * scale
    first_cross = jnp.where(zero, 0.0, 2.0 * only_x * col_sin) * scale
    lanes = jnp.concatenate
    same = lanes([same_re, same_im], axis=2)
    swap = lanes([cross, -cross], axis=2)
    first_same = lanes([first_re, first_im], axis=2)
    first_swap = lanes([first_cross, -first_cross], axis=2)
    return row_cos, row_sin, same, swap, first_same, first_swap


def send_kernel(rows, cores, table_left, fixed, table, dst, stage, send_sem, recv_sem, own_sem):
    count = rows * cores
    lanes = stage.shape[2]
    row, core = lax.axis_index("row"), lax.axis_index("epoch")
    me = row * cores + core
    barrier = pltpu.get_barrier_semaphore()

    def place(device):
        return {"row": lax.div(device, cores), "epoch": lax.rem(device, cores)}

    for step in range(1, count):
        pl.semaphore_signal(
            barrier,
            inc=1,
            device_id=place(lax.rem(me + step, count)),
            device_id_type=pl.DeviceIdType.MESH,
        )
    pl.semaphore_wait(barrier, count - 1)

    def remote(device, slot):
        return pltpu.make_async_remote_copy(
            src_ref=stage.at[device],
            dst_ref=dst.at[slot],
            send_sem=send_sem.at[device],
            recv_sem=recv_sem.at[slot],
            device_id=place(device),
            device_id_type=pl.DeviceIdType.MESH,
        )

    def multiply(chip):
        left, right = (table[chip], fixed[...]) if table_left else (fixed[...], table[chip])
        block = jnp.dot(left, right, preferred_element_type=jnp.float32).astype(stage.dtype)
        for other in range(cores):
            stage[chip * cores + other] = block[:, other * lanes : (other + 1) * lanes]

    def one_chip(step, carry):
        offset = rows // 2 + ((step + 1) // 2) * (2 * (step % 2) - 1)
        chip = lax.rem(row + offset, rows)
        multiply(chip)
        for other in range(cores):
            remote(chip * cores + other, me).start()
        return carry

    lax.fori_loop(0, rows - 1, one_chip, 0)
    multiply(row)
    for step in range(1, cores):
        remote(row * cores + lax.rem(core + step, cores), me).start()
    own = pltpu.make_async_copy(stage.at[me], dst.at[me], own_sem)
    own.start()
    own.wait()

    def finish(step, carry):
        device = lax.rem(me + step, count)
        remote(device, device).wait()
        return carry

    lax.fori_loop(1, count, finish, 0)


def multiply_and_send(fixed, table, rows, cores, table_left, identity):
    height = table.shape[1] if table_left else fixed.shape[0]
    width = (fixed.shape[1] if table_left else table.shape[2]) // cores
    shape = (rows * cores, height, width)
    return pl.pallas_call(
        functools.partial(send_kernel, rows, cores, table_left),
        out_shape=jax.ShapeDtypeStruct(shape, jnp.bfloat16),
        in_specs=[pl.BlockSpec(memory_space=pltpu.VMEM)] * 2,
        out_specs=pl.BlockSpec(memory_space=pl.ANY),
        scratch_shapes=[
            pltpu.VMEM(shape, jnp.bfloat16),
            pltpu.SemaphoreType.DMA((rows * cores,)),
            pltpu.SemaphoreType.DMA((rows * cores,)),
            pltpu.SemaphoreType.DMA,
        ],
        compiler_params=pltpu.CompilerParams(
            collective_id=identity, has_side_effects=True, vmem_limit_bytes=40 * 2**20
        ),
    )(fixed, table)


def exchange(blocks):
    return lax.all_to_all(blocks, ("row", "epoch"), split_axis=0, concat_axis=0, tiled=True)


def local(images, rate_vectors, epoch_times):
    loc_epochs, loc_rows, length = images.shape
    row_count = lax.axis_size("row")
    epoch_count = lax.axis_size("epoch")
    devices = row_count * epoch_count
    place = lax.axis_index("row") * epoch_count + lax.axis_index("epoch")
    lanes = length // devices
    slots = lanes // 2
    half = length // 2
    rates = rate_vectors.shape[0]
    table = real_table(length)
    lane_table = table[lane_order(length, devices)]
    rowwise = jnp.asarray(np.ascontiguousarray(lane_table.T))
    inverse = jnp.asarray(lane_table).reshape(devices, lanes, length)
    forward = jnp.asarray(table)
    fused = lanes % 128 == 0 and loc_rows % 16 == 0 and rates == epoch_count and row_count % 2 == 0
    if fused:
        chips = lane_table.T.reshape(length, row_count, epoch_count * lanes).transpose(1, 0, 2)
        chips = jnp.asarray(np.ascontiguousarray(chips))
        flat = images.reshape(loc_epochs * loc_rows, length)
        got = multiply_and_send(flat, chips, row_count, epoch_count, False, 0)
    else:
        spectrum = jnp.einsum("erc,cl->erl", images, rowwise, preferred_element_type=jnp.float32)
        spectrum = spectrum.astype(jnp.bfloat16).reshape(loc_epochs, loc_rows, devices, lanes)
        got = exchange(spectrum.transpose(2, 0, 1, 3))
    got = got.reshape(row_count, epoch_count * loc_epochs, loc_rows, lanes)
    pairs = jnp.einsum(
        "uir,ierl->eul",
        forward.reshape(length, row_count, loc_rows),
        got,
        preferred_element_type=jnp.float32,
    )
    row_cos, row_sin, same, swap, first_same, first_swap = coefficients(
        rate_vectors, epoch_times, place * slots, slots, length
    )
    even, odd = pairs[:, :half], pairs[:, half:]
    swapped = lambda a: jnp.concatenate([a[..., slots:], a[..., :slots]], axis=-1)
    row_cos, row_sin = row_cos[..., None], row_sin[..., None]
    moved_even = row_cos * even[None] + row_sin * odd[None]
    moved_odd = row_cos * odd[None] - row_sin * even[None]
    first = (jnp.arange(half) == 0)[None, None, :, None]
    same_even = jnp.where(first, first_same[:, :, None], same[:, :, None])
    swap_even = jnp.where(first, first_swap[:, :, None], swap[:, :, None])
    sum_even = jnp.sum(same_even * moved_even + swap_even * swapped(moved_even), axis=1)
    sum_odd = jnp.sum(same[:, :, None] * moved_odd + swap[:, :, None] * swapped(moved_odd), axis=1)
    stacked = jnp.concatenate([sum_even, sum_odd], axis=1).astype(jnp.bfloat16)
    if fused:
        chips = table.T.reshape(row_count, loc_rows, length)
        chips = jnp.asarray(np.ascontiguousarray(chips))
        flat = stacked.transpose(1, 0, 2).reshape(length, rates * lanes)
        returned = multiply_and_send(flat, chips, row_count, epoch_count, True, 1)
        returned = returned[:, None]
    else:
        back = jnp.einsum("ur,kul->krl", forward, stacked, preferred_element_type=jnp.float32)
        back = back.astype(jnp.bfloat16)
        back = back.reshape(epoch_count, rates // epoch_count, row_count, loc_rows, lanes)
        back = back.transpose(2, 0, 1, 3, 4)
        returned = exchange(back.reshape(devices, rates // epoch_count, loc_rows, lanes))
    return jnp.einsum("dkrl,dlc->krc", returned, inverse, preferred_element_type=jnp.float32)


def solution(mesh):
    in_specs = (P(("group", "epoch"), "row", None), P(), P())
    out_specs = P(("group", "epoch"), "row", None)
    return jax.shard_map(local, mesh=mesh, in_specs=in_specs, out_specs=out_specs, check_vma=False)
```

```python
import functools
import math

import jax
import jax.numpy as jnp
import ml_dtypes
import numpy as np
from jax import lax
from jax.experimental import pallas as pl
from jax.experimental.pallas import tpu as pltpu
from jax.sharding import PartitionSpec as P

SUBPIX = 16


@functools.lru_cache(maxsize=None)
def real_table(length):
    half = length // 2
    positions = np.arange(length, dtype=np.int64)
    turns = (positions[:half, None] * positions[None, :]) % length
    angles = turns * (2.0 * math.pi / length)
    factor = 1.0 / math.sqrt(length)
    nyquist = 1.0 - 2.0 * (positions % 2)
    table = np.concatenate([np.cos(angles), nyquist[None], np.sin(angles)[1:]]) * factor
    return table.astype(np.float32).astype(ml_dtypes.bfloat16)


def lane_order(length, devices):
    half = length // 2
    slots = np.arange(half).reshape(devices, 1, half // devices)
    return np.concatenate([slots, slots + half], axis=1).reshape(-1)


def turn_cos_sin(turns, period):
    angles = (turns % period).astype(jnp.float32) * (2.0 * math.pi / period)
    return jnp.cos(angles), jnp.sin(angles)


def coefficients(rate_vectors, epoch_times, first_slot, slots, length):
    period = SUBPIX * length
    half = length // 2
    scale = 1.0 / math.sqrt(epoch_times.shape[0])
    shift_y = rate_vectors[:, 0:1] * epoch_times[None, :] % period
    shift_x = rate_vectors[:, 1:2] * epoch_times[None, :] % period
    freq = jnp.arange(half, dtype=jnp.int32)
    row_cos, row_sin = turn_cos_sin((freq - half) * shift_y[:, :, None], period)
    row_cos = jnp.where(freq == 0, 1.0, 2.0 * row_cos)
    row_sin = jnp.where(freq == 0, 0.0, 2.0 * row_sin)
    slot = first_slot + jnp.arange(slots, dtype=jnp.int32)
    col_cos, col_sin = turn_cos_sin((slot - half) * shift_x[:, :, None], period)
    both = turn_cos_sin(shift_y + shift_x, 2 * SUBPIX)[0][:, :, None]
    only_y = turn_cos_sin(shift_y, 2 * SUBPIX)[0][:, :, None]
    only_x = turn_cos_sin(shift_x, 2 * SUBPIX)[0][:, :, None]
    zero = slot == 0
    same_re = jnp.where(zero, only_y, 2.0 * both * col_cos) * scale
    same_im = jnp.where(zero, both, 2.0 * both * col_cos) * scale
    cross = jnp.where(zero, 0.0, 2.0 * both * col_sin) * scale
    first_re = jnp.where(zero, 1.0, 2.0 * only_x * col_cos) * scale
    first_im = jnp.where(zero, only_x, 2.0 * only_x * col_cos) * scale
    first_cross = jnp.where(zero, 0.0, 2.0 * only_x * col_sin) * scale
    lanes = jnp.concatenate
    same = lanes([same_re, same_im], axis=2)
    swap = lanes([cross, -cross], axis=2)
    first_same = lanes([first_re, first_im], axis=2)
    first_swap = lanes([first_cross, -first_cross], axis=2)
    return row_cos, row_sin, same, swap, first_same, first_swap


def send_kernel(
    rows, cores, table_left, fixed, source, dst, stage, table, load_sem, send_sem, recv_sem, own_sem
):
    count = rows * cores
    lanes = stage.shape[2]
    row, core = lax.axis_index("row"), lax.axis_index("epoch")
    me = row * cores + core

    def chip_at(step):
        offset = rows // 2 + ((step + 1) // 2) * (2 * (step % 2) - 1)
        return lax.rem(row + offset, rows)

    def load(chip):
        return pltpu.make_async_copy(source.at[chip], table.at[chip], load_sem.at[chip])

    def start_load(step, carry):
        load(chip_at(step)).start()
        return carry

    lax.fori_loop(0, rows, start_load, 0)
    barrier = pltpu.get_barrier_semaphore()

    def place(device):
        return {"row": lax.div(device, cores), "epoch": lax.rem(device, cores)}

    for step in range(1, count):
        pl.semaphore_signal(
            barrier,
            inc=1,
            device_id=place(lax.rem(me + step, count)),
            device_id_type=pl.DeviceIdType.MESH,
        )
    pl.semaphore_wait(barrier, count - 1)

    def remote(device, slot):
        return pltpu.make_async_remote_copy(
            src_ref=stage.at[device],
            dst_ref=dst.at[slot],
            send_sem=send_sem.at[device],
            recv_sem=recv_sem.at[slot],
            device_id=place(device),
            device_id_type=pl.DeviceIdType.MESH,
        )

    def multiply(chip):
        load(chip).wait()
        left, right = (table[chip], fixed[...]) if table_left else (fixed[...], table[chip])
        block = jnp.dot(left, right, preferred_element_type=jnp.float32).astype(stage.dtype)
        for other in range(cores):
            stage[chip * cores + other] = block[:, other * lanes : (other + 1) * lanes]

    def one_chip(step, carry):
        chip = chip_at(step)
        multiply(chip)
        for other in range(cores):
            remote(chip * cores + other, me).start()
        return carry

    lax.fori_loop(0, rows - 1, one_chip, 0)
    multiply(row)
    for step in range(1, cores):
        remote(row * cores + lax.rem(core + step, cores), me).start()
    own = pltpu.make_async_copy(stage.at[me], dst.at[me], own_sem)
    own.start()
    own.wait()

    def finish(step, carry):
        device = lax.rem(me + step, count)
        remote(device, device).wait()
        return carry

    lax.fori_loop(1, count, finish, 0)


def multiply_and_send(fixed, table, rows, cores, table_left, identity):
    height = table.shape[1] if table_left else fixed.shape[0]
    width = (fixed.shape[1] if table_left else table.shape[2]) // cores
    shape = (rows * cores, height, width)
    return pl.pallas_call(
        functools.partial(send_kernel, rows, cores, table_left),
        out_shape=jax.ShapeDtypeStruct(shape, jnp.bfloat16),
        in_specs=[
            pl.BlockSpec(memory_space=pltpu.VMEM),
            pl.BlockSpec(memory_space=pl.ANY),
        ],
        out_specs=pl.BlockSpec(memory_space=pl.ANY),
        scratch_shapes=[
            pltpu.VMEM(shape, jnp.bfloat16),
            pltpu.VMEM(table.shape, jnp.bfloat16),
            pltpu.SemaphoreType.DMA((rows,)),
            pltpu.SemaphoreType.DMA((rows * cores,)),
            pltpu.SemaphoreType.DMA((rows * cores,)),
            pltpu.SemaphoreType.DMA,
        ],
        compiler_params=pltpu.CompilerParams(
            collective_id=identity, has_side_effects=True, vmem_limit_bytes=56 * 2**20
        ),
    )(fixed, table)


def exchange(blocks):
    return lax.all_to_all(blocks, ("row", "epoch"), split_axis=0, concat_axis=0, tiled=True)


def local(images, rate_vectors, epoch_times):
    loc_epochs, loc_rows, length = images.shape
    row_count = lax.axis_size("row")
    epoch_count = lax.axis_size("epoch")
    devices = row_count * epoch_count
    place = lax.axis_index("row") * epoch_count + lax.axis_index("epoch")
    lanes = length // devices
    slots = lanes // 2
    half = length // 2
    rates = rate_vectors.shape[0]
    table = real_table(length)
    lane_table = table[lane_order(length, devices)]
    rowwise = jnp.asarray(np.ascontiguousarray(lane_table.T))
    inverse = jnp.asarray(lane_table).reshape(devices, lanes, length)
    forward = jnp.asarray(table)
    fused = lanes % 128 == 0 and loc_rows % 16 == 0 and rates == epoch_count and row_count % 2 == 0
    if fused:
        chips = lane_table.T.reshape(length, row_count, epoch_count * lanes).transpose(1, 0, 2)
        chips = jnp.asarray(np.ascontiguousarray(chips))
        flat = images.reshape(loc_epochs * loc_rows, length)
        got = multiply_and_send(flat, chips, row_count, epoch_count, False, 0)
    else:
        spectrum = jnp.einsum("erc,cl->erl", images, rowwise, preferred_element_type=jnp.float32)
        spectrum = spectrum.astype(jnp.bfloat16).reshape(loc_epochs, loc_rows, devices, lanes)
        got = exchange(spectrum.transpose(2, 0, 1, 3))
    got = got.reshape(row_count, epoch_count * loc_epochs, loc_rows, lanes)
    pairs = jnp.einsum(
        "uir,ierl->eul",
        forward.reshape(length, row_count, loc_rows),
        got,
        preferred_element_type=jnp.float32,
    )
    row_cos, row_sin, same, swap, first_same, first_swap = coefficients(
        rate_vectors, epoch_times, place * slots, slots, length
    )
    even, odd = pairs[:, :half], pairs[:, half:]
    swapped = lambda a: jnp.concatenate([a[..., slots:], a[..., :slots]], axis=-1)
    row_cos, row_sin = row_cos[..., None], row_sin[..., None]
    moved_even = row_cos * even[None] + row_sin * odd[None]
    moved_odd = row_cos * odd[None] - row_sin * even[None]
    first = (jnp.arange(half) == 0)[None, None, :, None]
    same_even = jnp.where(first, first_same[:, :, None], same[:, :, None])
    swap_even = jnp.where(first, first_swap[:, :, None], swap[:, :, None])
    sum_even = jnp.sum(same_even * moved_even + swap_even * swapped(moved_even), axis=1)
    sum_odd = jnp.sum(same[:, :, None] * moved_odd + swap[:, :, None] * swapped(moved_odd), axis=1)
    stacked = jnp.concatenate([sum_even, sum_odd], axis=1).astype(jnp.bfloat16)
    if fused:
        chips = table.T.reshape(row_count, loc_rows, length)
        chips = jnp.asarray(np.ascontiguousarray(chips))
        flat = stacked.transpose(1, 0, 2).reshape(length, rates * lanes)
        returned = multiply_and_send(flat, chips, row_count, epoch_count, True, 1)
        returned = returned[:, None]
    else:
        back = jnp.einsum("ur,kul->krl", forward, stacked, preferred_element_type=jnp.float32)
        back = back.astype(jnp.bfloat16)
        back = back.reshape(epoch_count, rates // epoch_count, row_count, loc_rows, lanes)
        back = back.transpose(2, 0, 1, 3, 4)
        returned = exchange(back.reshape(devices, rates // epoch_count, loc_rows, lanes))
    return jnp.einsum("dkrl,dlc->krc", returned, inverse, preferred_element_type=jnp.float32)


def solution(mesh):
    in_specs = (P(("group", "epoch"), "row", None), P(), P())
    out_specs = P(("group", "epoch"), "row", None)
    return jax.shard_map(local, mesh=mesh, in_specs=in_specs, out_specs=out_specs, check_vma=False)
```

```python
import functools
import math

import jax
import jax.numpy as jnp
import ml_dtypes
import numpy as np
from jax import lax
from jax.experimental import pallas as pl
from jax.experimental.pallas import tpu as pltpu
from jax.sharding import PartitionSpec as P

SUBPIX = 16


@functools.lru_cache(maxsize=None)
def real_table(length):
    half = length // 2
    positions = np.arange(length, dtype=np.int64)
    turns = (positions[:half, None] * positions[None, :]) % length
    angles = turns * (2.0 * math.pi / length)
    factor = 1.0 / math.sqrt(length)
    nyquist = 1.0 - 2.0 * (positions % 2)
    table = np.concatenate([np.cos(angles), nyquist[None], np.sin(angles)[1:]]) * factor
    return table.astype(np.float32).astype(ml_dtypes.bfloat16)


def lane_order(length, devices):
    half = length // 2
    slots = np.arange(half).reshape(devices, 1, half // devices)
    return np.concatenate([slots, slots + half], axis=1).reshape(-1)


def turn_cos_sin(turns, period):
    angles = (turns % period).astype(jnp.float32) * (2.0 * math.pi / period)
    return jnp.cos(angles), jnp.sin(angles)


def coefficients(rate_vectors, epoch_times, first_slot, slots, length):
    period = SUBPIX * length
    half = length // 2
    scale = 1.0 / math.sqrt(epoch_times.shape[0])
    shift_y = rate_vectors[:, 0:1] * epoch_times[None, :] % period
    shift_x = rate_vectors[:, 1:2] * epoch_times[None, :] % period
    freq = jnp.arange(half, dtype=jnp.int32)
    row_cos, row_sin = turn_cos_sin((freq - half) * shift_y[:, :, None], period)
    row_cos = jnp.where(freq == 0, 1.0, 2.0 * row_cos)
    row_sin = jnp.where(freq == 0, 0.0, 2.0 * row_sin)
    slot = first_slot + jnp.arange(slots, dtype=jnp.int32)
    col_cos, col_sin = turn_cos_sin((slot - half) * shift_x[:, :, None], period)
    both = turn_cos_sin(shift_y + shift_x, 2 * SUBPIX)[0][:, :, None]
    only_y = turn_cos_sin(shift_y, 2 * SUBPIX)[0][:, :, None]
    only_x = turn_cos_sin(shift_x, 2 * SUBPIX)[0][:, :, None]
    zero = slot == 0
    same_re = jnp.where(zero, only_y, 2.0 * both * col_cos) * scale
    same_im = jnp.where(zero, both, 2.0 * both * col_cos) * scale
    cross = jnp.where(zero, 0.0, 2.0 * both * col_sin) * scale
    first_re = jnp.where(zero, 1.0, 2.0 * only_x * col_cos) * scale
    first_im = jnp.where(zero, only_x, 2.0 * only_x * col_cos) * scale
    first_cross = jnp.where(zero, 0.0, 2.0 * only_x * col_sin) * scale
    lanes = jnp.concatenate
    same = lanes([same_re, same_im], axis=2)
    swap = lanes([cross, -cross], axis=2)
    first_same = lanes([first_re, first_im], axis=2)
    first_swap = lanes([first_cross, -first_cross], axis=2)
    return row_cos, row_sin, same, swap, first_same, first_swap


def send_kernel(
    rows, cores, table_left, fixed, source, dst, stage, table, load_sem, send_sem, recv_sem, own_sem
):
    count = rows * cores
    lanes = stage.shape[2]
    row, core = lax.axis_index("row"), lax.axis_index("epoch")
    me = row * cores + core

    def chip_at(step):
        offset = rows // 2 + ((step + 1) // 2) * (2 * (step % 2) - 1)
        return lax.rem(row + offset, rows)

    def load(chip):
        return pltpu.make_async_copy(source.at[chip], table.at[chip], load_sem.at[chip])

    def start_load(step, carry):
        load(chip_at(step)).start()
        return carry

    lax.fori_loop(0, rows, start_load, 0)
    barrier = pltpu.get_barrier_semaphore()

    def place(device):
        return {"row": lax.div(device, cores), "epoch": lax.rem(device, cores)}

    for step in range(1, count):
        pl.semaphore_signal(
            barrier,
            inc=1,
            device_id=place(lax.rem(me + step, count)),
            device_id_type=pl.DeviceIdType.MESH,
        )
    pl.semaphore_wait(barrier, count - 1)

    def remote(device, slot):
        return pltpu.make_async_remote_copy(
            src_ref=stage.at[device],
            dst_ref=dst.at[slot],
            send_sem=send_sem.at[device],
            recv_sem=recv_sem.at[slot],
            device_id=place(device),
            device_id_type=pl.DeviceIdType.MESH,
        )

    def multiply(chip):
        load(chip).wait()
        left, right = (table[chip], fixed[...]) if table_left else (fixed[...], table[chip])
        block = jnp.dot(left, right, preferred_element_type=jnp.float32).astype(stage.dtype)
        for other in range(cores):
            stage[chip * cores + other] = block[:, other * lanes : (other + 1) * lanes]

    def one_chip(step, carry):
        chip = chip_at(step)
        multiply(chip)
        for other in range(cores):
            remote(chip * cores + other, me).start()
        return carry

    lax.fori_loop(0, rows - 1, one_chip, 0)
    multiply(row)
    for step in range(1, cores):
        remote(row * cores + lax.rem(core + step, cores), me).start()
    own = pltpu.make_async_copy(stage.at[me], dst.at[me], own_sem)
    own.start()
    own.wait()

    def finish(step, carry):
        device = lax.rem(me + step, count)
        remote(device, device).wait()
        return carry

    lax.fori_loop(1, count, finish, 0)


def multiply_and_send(fixed, table, rows, cores, table_left, identity):
    height = table.shape[1] if table_left else fixed.shape[0]
    width = (fixed.shape[1] if table_left else table.shape[2]) // cores
    shape = (rows * cores, height, width)
    return pl.pallas_call(
        functools.partial(send_kernel, rows, cores, table_left),
        out_shape=jax.ShapeDtypeStruct(shape, jnp.bfloat16),
        in_specs=[
            pl.BlockSpec(memory_space=pltpu.VMEM),
            pl.BlockSpec(memory_space=pl.ANY),
        ],
        out_specs=pl.BlockSpec(memory_space=pl.ANY),
        scratch_shapes=[
            pltpu.VMEM(shape, jnp.bfloat16),
            pltpu.VMEM(table.shape, jnp.bfloat16),
            pltpu.SemaphoreType.DMA((rows,)),
            pltpu.SemaphoreType.DMA((rows * cores,)),
            pltpu.SemaphoreType.DMA((rows * cores,)),
            pltpu.SemaphoreType.DMA,
        ],
        compiler_params=pltpu.CompilerParams(
            collective_id=identity, has_side_effects=True, vmem_limit_bytes=50 * 2**20
        ),
    )(fixed, table)


def exchange(blocks):
    return lax.all_to_all(blocks, ("row", "epoch"), split_axis=0, concat_axis=0, tiled=True)


def local(images, rate_vectors, epoch_times):
    loc_epochs, loc_rows, length = images.shape
    row_count = lax.axis_size("row")
    epoch_count = lax.axis_size("epoch")
    devices = row_count * epoch_count
    place = lax.axis_index("row") * epoch_count + lax.axis_index("epoch")
    lanes = length // devices
    slots = lanes // 2
    half = length // 2
    rates = rate_vectors.shape[0]
    table = real_table(length)
    lane_table = table[lane_order(length, devices)]
    rowwise = jnp.asarray(np.ascontiguousarray(lane_table.T))
    inverse = jnp.asarray(lane_table).reshape(devices, lanes, length)
    forward = jnp.asarray(table)
    fused = lanes % 128 == 0 and loc_rows % 16 == 0 and rates == epoch_count and row_count % 2 == 0
    if fused:
        chips = lane_table.T.reshape(length, row_count, epoch_count * lanes).transpose(1, 0, 2)
        chips = jnp.asarray(np.ascontiguousarray(chips))
        flat = images.reshape(loc_epochs * loc_rows, length)
        got = multiply_and_send(flat, chips, row_count, epoch_count, False, 0)
    else:
        spectrum = jnp.einsum("erc,cl->erl", images, rowwise, preferred_element_type=jnp.float32)
        spectrum = spectrum.astype(jnp.bfloat16).reshape(loc_epochs, loc_rows, devices, lanes)
        got = exchange(spectrum.transpose(2, 0, 1, 3))
    got = got.reshape(row_count, epoch_count * loc_epochs, loc_rows, lanes)
    pairs = jnp.einsum(
        "uir,ierl->eul",
        forward.reshape(length, row_count, loc_rows),
        got,
        preferred_element_type=jnp.float32,
    )
    row_cos, row_sin, same, swap, first_same, first_swap = coefficients(
        rate_vectors, epoch_times, place * slots, slots, length
    )
    even, odd = pairs[:, :half], pairs[:, half:]
    swapped = lambda a: jnp.concatenate([a[..., slots:], a[..., :slots]], axis=-1)
    row_cos, row_sin = row_cos[..., None], row_sin[..., None]
    moved_even = row_cos * even[None] + row_sin * odd[None]
    moved_odd = row_cos * odd[None] - row_sin * even[None]
    first = (jnp.arange(half) == 0)[None, None, :, None]
    same_even = jnp.where(first, first_same[:, :, None], same[:, :, None])
    swap_even = jnp.where(first, first_swap[:, :, None], swap[:, :, None])
    sum_even = jnp.sum(same_even * moved_even + swap_even * swapped(moved_even), axis=1)
    sum_odd = jnp.sum(same[:, :, None] * moved_odd + swap[:, :, None] * swapped(moved_odd), axis=1)
    stacked = jnp.concatenate([sum_even, sum_odd], axis=1).astype(jnp.bfloat16)
    if fused:
        chips = table.T.reshape(row_count, loc_rows, length)
        chips = jnp.asarray(np.ascontiguousarray(chips))
        flat = stacked.transpose(1, 0, 2).reshape(length, rates * lanes)
        returned = multiply_and_send(flat, chips, row_count, epoch_count, True, 1)
        returned = returned[:, None]
    else:
        back = jnp.einsum("ur,kul->krl", forward, stacked, preferred_element_type=jnp.float32)
        back = back.astype(jnp.bfloat16)
        back = back.reshape(epoch_count, rates // epoch_count, row_count, loc_rows, lanes)
        back = back.transpose(2, 0, 1, 3, 4)
        returned = exchange(back.reshape(devices, rates // epoch_count, loc_rows, lanes))
    return jnp.einsum("dkrl,dlc->krc", returned, inverse, preferred_element_type=jnp.float32)


def solution(mesh):
    in_specs = (P(("group", "epoch"), "row", None), P(), P())
    out_specs = P(("group", "epoch"), "row", None)
    return jax.shard_map(local, mesh=mesh, in_specs=in_specs, out_specs=out_specs, check_vma=False)
```
